512 devices in a mesh: ia: 16 (over y_hi, x), ja: 16 (over z, core), vert: 2 (over y_lo).
Axes of the slice: x: 4, y: 8 (y_hi: 4, y_lo: 2; y = y_hi * 2 + y_lo), z: 8, core: 2. Of those that a mesh axis runs over, the one named last changes fastest.
Arguments:
- amplitudes: bfloat16 [16, 16, 2, 2, 3, 16384], P('ia', 'ja'), may hold values from -6 to 6
- tile_lists: int32 [16, 16, 3], P('ia', 'ja'), may hold values from 0 to 3, as said below
- integrals: bfloat16 [32, 256, 256], P('ia', 'vert'), may hold values from -0.1875 to 0.1875
- occupied_energy: float32 [32], replicated, may hold values from -2 to -0.5
- virtual_energy: float32 [256], replicated, may hold values from 0.5 to 4
Outputs:
- ladder_update: bfloat16 [16, 16, 2, 2, 256, 256], P('ia', 'ja', None, None, 'vert')
The draws below stay inside these ranges and needn't reach their ends.
Inputs may be any that keep to these rules, and one draw needn't show every extreme that they name: `tile_lists`: the 3 entries of one pair block are distinct.
All inputs are finite; a program needn't handle non-finite values.
Results may differ from the reference program's by a relative error of at most 0.0049.
Values may be sent and summed in bfloat16 or wider, within the bound.
A program may use at most 64 MiB of HBM per device.

```python
import jax
import jax.numpy as jnp
from jax import lax

OI = 2
VB = 128
NT = 2
KT = 3
NQ = 32
NV = 256
TILE2 = 16384
OCC_TILES = 16
NOCC = 32


def draw_tile_lists(key, part):
    key = jax.random.fold_in(key, 11)
    scores = jax.random.randint(key, (OCC_TILES, OCC_TILES, NT * NT), 0, 2 ** 20)
    scores = scores * (NT * NT) + jnp.arange(NT * NT, dtype=jnp.int32)
    ranking = jnp.argsort(scores, axis=-1, stable=True)
    return ranking[..., :KT].astype(jnp.int32)


def steps_of(own_key, shape, pieces, low, high):
    level, own = 1.0, jax.random.fold_in(own_key, 6)
    for dim, blocks in pieces:
        steps = jnp.exp(jax.random.uniform(jax.random.fold_in(own, dim), (blocks,), jnp.float32, low / len(pieces), high / len(pieces)))
        level = level * jnp.repeat(steps, shape[dim] // blocks).reshape([-1 if axis == dim else 1 for axis in range(len(shape))])
    return level


def gaussian(rng, shape, width, bound, pieces=(), kind=jnp.bfloat16):
    values = width * jax.random.normal(rng, shape, jnp.float32)
    if pieces:
        values = values * steps_of(rng, shape, pieces, -0.22, 0.18)
    return jnp.clip(values, -bound, bound).astype(kind)


def setup_inputs(seed: int = 0) -> dict:
    seeds = jax.random.split(jax.random.key(seed), 6)
    amplitudes = gaussian(seeds[0], (OCC_TILES, OCC_TILES, OI, OI, KT, TILE2), 1.0, 6.0, ((0, 16), (1, 16)))
    tile_lists = draw_tile_lists(jax.random.fold_in(seeds[5], 71), 0)
    integrals = gaussian(seeds[2], (NQ, NV, NV), (NV * 4) ** -0.5, 0.1875, ((0, 16), (1, 2)))
    occupied_energy = jnp.clip(jax.random.uniform(seeds[3], (NOCC,), jnp.float32, -2.0, -0.5), -2.0, -0.5)
    virtual_energy = jnp.clip(jax.random.uniform(seeds[4], (NV,), jnp.float32, 0.5, 4.0), 0.5, 4.0)
    return dict(amplitudes=amplitudes, tile_lists=tile_lists, integrals=integrals, occupied_energy=occupied_energy, virtual_energy=virtual_energy)


def reference(amplitudes, tile_lists, integrals, occupied_energy, virtual_energy):
    grid = OCC_TILES
    pair_count = OI * OI
    flat_amps = amplitudes.reshape(grid * grid, pair_count, KT, TILE2)
    flat_lists = tile_lists.reshape(grid * grid, KT).astype(jnp.int32)
    tile_ids = jnp.arange(NT * NT, dtype=jnp.int32)
    factors = integrals.astype(jnp.float32)

    def ladder_block(inputs):
        amp_block, list_block = inputs
        catalog = (list_block[:, None] == tile_ids[None, :]).astype(jnp.float32)
        dense = jnp.einsum("pkt,ks->pst", amp_block.astype(jnp.float32), catalog,
                           precision=lax.Precision.HIGHEST)
        dense = dense.reshape(pair_count, NT, NT, VB, VB).transpose(0, 1, 3, 2, 4).reshape(pair_count, NV, NV)

        def one_factor(total, factor):
            inner = jnp.einsum("pcd,bd->pcb", dense, factor, precision=lax.Precision.HIGHEST)
            inner = lax.optimization_barrier(inner.astype(jnp.bfloat16)).astype(jnp.float32)
            return total + jnp.einsum("ac,pcb->pab", factor, inner, precision=lax.Precision.HIGHEST), None

        total, _ = lax.scan(one_factor, jnp.zeros((pair_count, NV, NV), jnp.float32), factors)
        return total

    ladder = lax.map(ladder_block, (flat_amps, flat_lists))
    grid_ids = jnp.arange(grid * grid, dtype=jnp.int32)
    mirror_index = jnp.bitwise_xor(grid_ids // grid, grid_ids % grid) * grid + grid_ids % grid
    occ_rows = occupied_energy.reshape(grid, OI)

    def finish(index):
        own = ladder[index].reshape(OI, OI, NV, NV)
        other = ladder[mirror_index[index]].reshape(OI, OI, NV, NV).transpose(1, 0, 3, 2)
        summed = own + other
        row_tile = index // grid
        code_tile = index % grid
        occ_i = occ_rows[row_tile]
        occ_j = occ_rows[jnp.bitwise_xor(row_tile, code_tile)]
        denom = (virtual_energy[None, None, :, None] + virtual_energy[None, None, None, :]) - (
            occ_i[:, None, None, None] + occ_j[None, :, None, None])
        return (summed / denom).astype(jnp.bfloat16)

    result = lax.map(finish, grid_ids)
    return result.reshape(grid, grid, OI, OI, NV, NV)
```

```python
import jax
import jax.numpy as jnp
from jax import lax
from jax.experimental import pallas as pl
from jax.experimental.pallas import tpu as pltpu
from jax.sharding import PartitionSpec as P

NX, NY, NZ = 4, 8, 8
NT = 2
VB = 128
KT = 3
ROWS = 64
WIDE = 256
PAIRS = 4
MESH = pl.DeviceIdType.MESH
ROWS_BY_ROWS = (((1,), (1,)), ((), ()))


def xor(a, b, bits):
    total = 0
    for level in range(bits):
        unit = 2**level
        total = total + (a // unit % 2 + b // unit % 2) % 2 * unit
    return total


def kernel(
    ints, amps, codes, out, buf, inner, dense, mirror, mirror_codes,
    ysend, yrecv, xsend, xrecv, zsend, zrecv, csend, crecv, msend, mrecv, vsend, vrecv,
):
    ia, ja, v = lax.axis_index("ia"), lax.axis_index("ja"), lax.axis_index("vert")
    x, y = ia % NX, ia // NX * 2 + v
    z, core = ja // 2, ja % 2
    zp = z % 2

    def device(x_at, y_at, z_at, core_at):
        return (y_at // 2 * NX + x_at, z_at * 2 + core_at, y_at % 2)

    left, right, across = (x + 3) % NX, (x + 1) % NX, (x + 2) % NX
    to_left, to_right = device(left, y, z, core), device(right, y, z, core)
    to_down, to_up = device(x, y, (z + NZ - 1) % NZ, core), device(x, y, (z + 1) % NZ, core)
    to_core = device(x, y, z, 1 - core)
    to_vert = (ia, ja, 1 - v)
    to_mirror = (xor(ia, ja, 4), ja, v)
    to_column = [device(x, (y + d) % NY, z, core) for d in range(1, NY)]
    has_mirror = ja > 0

    def send(src, dst, send_sem, recv_sem, target):
        return pltpu.make_async_remote_copy(
            src_ref=src, dst_ref=dst, send_sem=send_sem, recv_sem=recv_sem,
            device_id=target, device_id_type=MESH,
        )

    barrier = pltpu.get_barrier_semaphore()
    for peer in [to_left, to_right, to_down, to_up, to_core, *to_column]:
        pl.semaphore_signal(barrier, inc=1, device_id=peer, device_id_type=MESH)

    @pl.when(has_mirror)
    def _():
        pl.semaphore_signal(barrier, inc=1, device_id=to_mirror, device_id_type=MESH)
        pl.semaphore_wait(barrier, 5 + NY)

    @pl.when(jnp.logical_not(has_mirror))
    def _():
        pl.semaphore_wait(barrier, 5 + NY - 1)

    share = 2 * zp + core
    other_share = 2 * (1 - zp) + core
    groups = [x, left, right, across]
    mine = ints.at[core, pl.ds(pl.multiple_of(zp * ROWS, ROWS), ROWS), :]

    column = [
        send(mine, buf.at[share, x, y], ysend.at[d], yrecv.at[d], to_column[d])
        for d in range(NY - 1)
    ]
    for d in (0, 6, 1, 5, 2, 4, 3):
        column[d].start()

    def chunk(half, j):
        return mirror.at[pl.ds(half * 6 + 3 * j, 3)]

    over = [
        send(amps.at[pl.ds(v * 6 + 3 * j, 3)], chunk(v, j), msend.at[j], mrecv.at[j], to_mirror)
        for j in range(2)
    ]
    over_codes = send(codes, mirror_codes, msend.at[2], mrecv.at[2], to_mirror)
    aside = [send(chunk(v, j), chunk(v, j), vsend.at[j], vrecv.at[j], to_vert) for j in range(2)]

    @pl.when(has_mirror)
    def _():
        over_codes.start()
        for copy in over:
            copy.start()

    @pl.when(jnp.logical_not(has_mirror))
    def _():
        mirror[...] = amps[...]
        mirror_codes[...] = codes[...]

    buf[share, x, y] = mine[...]
    out[...] = jnp.zeros_like(out)

    def placed(tiles, listing, pair, tile):
        total = None
        for k in range(KT):
            factor = jnp.where(listing[k : k + 1, :] == tile, 1.0, 0.0).astype(jnp.bfloat16)
            term = tiles[pair * KT + k] * factor
            total = term if total is None else total + term
        return total

    def place(pair, c, d):
        return (slice(c * VB, (c + 1) * VB), slice(pair * WIDE + d * VB, pair * WIDE + (d + 1) * VB))

    for pair in range(PAIRS):
        for c in range(NT):
            for d in range(NT):
                dense[place(pair, c, d)] = placed(amps, codes, pair, c * NT + d)

    def part(which, n, h):
        return buf.at[which, groups[n], pl.ds(4 * h, 4)]

    def along(n, h, index, target):
        return send(part(share, n, h), part(share, n, h), xsend.at[index], xrecv.at[index], target)

    along_x = [
        along(0, 0, 0, to_right), along(0, 1, 1, to_right),
        along(0, 0, 2, to_left), along(0, 1, 3, to_left),
        along(1, 0, 4, to_right), along(2, 1, 5, to_left),
    ]
    along_z = [
        send(part(share, n, h), part(share, n, h), zsend.at[2 * n + h], zrecv.at[2 * n + h],
             to_up if h == 0 else to_down)
        for n in range(4) for h in range(2)
    ]
    along_c = [
        send(part(which, n, h), part(which, n, h), csend.at[4 * n + 2 * s + h],
             crecv.at[4 * n + 2 * s + h], to_core)
        for n in range(4) for s, which in enumerate((share, other_share)) for h in range(2)
    ]

    def spread(n, h):
        along_z[2 * n + h].start()
        along_c[4 * n + h].start()

    def pass_on(n):
        for h in range(2):
            along_z[2 * n + h].wait_recv()
            along_c[4 * n + 2 + h].start()

    for copy in column:
        copy.wait_recv()
    for index in (0, 3, 1, 2):
        along_x[index].start()
    spread(0, 0)
    spread(0, 1)

    @pl.when(has_mirror)
    def _():
        for j in range(2):
            over[j].wait_recv()
            aside[j].start()

    along_x[0].wait_recv()
    along_x[4].start()
    spread(1, 0)
    along_x[3].wait_recv()
    along_x[5].start()
    spread(2, 1)
    along_x[1].wait_recv()
    spread(1, 1)
    along_x[2].wait_recv()
    spread(2, 0)
    pass_on(0)

    @pl.when(has_mirror)
    def _():
        over_codes.wait_recv()
        for j in range(2):
            aside[j].wait_recv()

    for i in range(2):
        for j in range(2):
            for c in range(NT):
                for d in range(NT):
                    at = place(i * 2 + j, c, d)
                    turned = placed(mirror, mirror_codes, j * 2 + i, d * NT + c)
                    total = dense[at].astype(jnp.float32) + turned.astype(jnp.float32).T
                    dense[at] = total.astype(jnp.bfloat16)

    def ladder(n):
        g = groups[n]
        for q in range(0, 8, 2):
            k, first = q // 4, q % 4
            rows = []
            for hi in (first, first + 1):
                rows += [buf[k, g, 2 * hi + v], buf[2 + k, g, 2 * hi + v]]
            rows = jnp.concatenate(rows, axis=0)
            for pair in range(PAIRS):
                part_inner = jnp.dot(
                    rows, dense[:, pair * WIDE : (pair + 1) * WIDE],
                    preferred_element_type=jnp.float32,
                ).astype(jnp.bfloat16)
                for s in range(2):
                    inner[pair * VB : (pair + 1) * VB, (q + s) * WIDE : (q + s + 1) * WIDE] = (
                        part_inner[s * VB : (s + 1) * VB]
                    )
        factors = []
        for q in range(8):
            k, hi = q // 4, q % 4
            factors.append(
                jnp.concatenate(
                    [buf[k, g, 2 * hi], buf[2 + k, g, 2 * hi],
                     buf[k, g, 2 * hi + 1], buf[2 + k, g, 2 * hi + 1]], axis=0,
                )
            )
        out[...] += lax.dot_general(
            inner[...], jnp.concatenate(factors, axis=1), ROWS_BY_ROWS,
            preferred_element_type=jnp.float32,
        )

    def from_core(n):
        for index in range(4):
            along_c[4 * n + index].wait_recv()

    from_core(0)
    ladder(0)
    along_x[4].wait_recv()
    spread(3, 0)
    along_x[5].wait_recv()
    spread(3, 1)
    pass_on(1)
    pass_on(2)
    from_core(1)
    ladder(1)
    pass_on(3)
    from_core(2)
    ladder(2)
    from_core(3)
    ladder(3)

    for copy in [*column, *along_x, *along_z, *along_c]:
        copy.wait_send()

    @pl.when(has_mirror)
    def _():
        for copy in [*over, over_codes, *aside]:
            copy.wait_send()


def on_device(amplitudes, tile_lists, integrals, occupied_energy, virtual_energy):
    occ_tile = amplitudes.shape[2]
    half_rows, width = integrals.shape[1:]
    tiles = amplitudes.reshape(PAIRS * KT, VB, VB)
    codes = jnp.broadcast_to(tile_lists.reshape(KT, 1), (KT, 128))
    codes = jnp.concatenate([codes, jnp.full((8 - KT, 128), -1, jnp.int32)], axis=0)
    vmem = pl.BlockSpec(memory_space=pltpu.VMEM)
    dma = pltpu.SemaphoreType.DMA
    symmetrized = pl.pallas_call(
        kernel,
        out_shape=jax.ShapeDtypeStruct((PAIRS * half_rows, width), jnp.float32),
        in_specs=[vmem] * 3,
        out_specs=vmem,
        scratch_shapes=[
            pltpu.VMEM((4, NX, NY, ROWS, WIDE), jnp.bfloat16),
            pltpu.VMEM((PAIRS * VB, 8 * WIDE), jnp.bfloat16),
            pltpu.VMEM((WIDE, PAIRS * WIDE), jnp.bfloat16),
            pltpu.VMEM((PAIRS * KT, VB, VB), jnp.bfloat16),
            pltpu.VMEM((8, 128), jnp.int32),
            dma((7,)), dma((7,)), dma((6,)), dma((6,)), dma((8,)), dma((8,)),
            dma((16,)), dma((16,)), dma((3,)), dma((3,)), dma((2,)), dma((2,)),
        ],
        compiler_params=pltpu.CompilerParams(
            collective_id=0, has_side_effects=True, vmem_limit_bytes=32 * 1024 * 1024
        ),
        name="ladder",
    )(integrals, tiles, codes)
    parity = lax.axis_index("vert")
    row_tile, code_tile = lax.axis_index("ia"), lax.axis_index("ja")
    occ_i = lax.dynamic_slice_in_dim(occupied_energy, row_tile * occ_tile, occ_tile)
    occ_j = lax.dynamic_slice_in_dim(
        occupied_energy, jnp.bitwise_xor(row_tile, code_tile) * occ_tile, occ_tile
    )
    virt_rows = lax.dynamic_slice_in_dim(virtual_energy, parity * half_rows, half_rows)
    denom = (
        virt_rows[None, None, :, None]
        + virtual_energy[None, None, None, :]
        - (occ_i[:, None, None, None] + occ_j[None, :, None, None])
    )
    result = symmetrized.reshape(occ_tile, occ_tile, half_rows, width) / denom
    return result.reshape(1, 1, occ_tile, occ_tile, half_rows, width).astype(jnp.bfloat16)


def solution(mesh):
    return jax.shard_map(
        on_device,
        mesh=mesh,
        in_specs=(
            P("ia", "ja", None, None, None, None),
            P("ia", "ja", None),
            P("ia", "vert", None),
            P(),
            P(),
        ),
        out_specs=P("ia", "ja", None, None, "vert", None),
        check_vma=False,
    )
```

```python
import jax
import jax.numpy as jnp
from jax import lax
from jax.experimental import pallas as pl
from jax.experimental.pallas import tpu as pltpu
from jax.sharding import PartitionSpec as P

NX, NY = 4, 8
NT = 2
VB = 128
KT = 3
WIDE = 256
PAIRS = 4
HALF = VB // 2
MESH = pl.DeviceIdType.MESH
ROWS_BY_ROWS = (((1,), (1,)), ((), ()))

STAGES = [(0,), (1, 4), (2, 5), (3, 6), (7,)]
ORDER = [
    ("column", 0), ("relayout", None), ("mirror", 0), ("mirror", 1), ("prepare", None), ("column", 1),
    ("mirror", 2), ("sides", 0), ("column", 2), ("sides", 1), ("forward", 0), ("across", 0), ("column", 3),
    ("forward", 1), ("sides", 2), ("forward", 2), ("across", 1), ("column", 4), ("core", 0), ("core", 1),
    ("symmetrize", 0), ("ladder", 0), ("sides", 3), ("across", 2), ("core", 2), ("ladder", 2), ("sides", 4),
    ("symmetrize", 1), ("ladder", 1), ("across", 3), ("ladder", 3), ("across", 4), ("core", 3),
    ("ladder", 4), ("ladder", 5), ("ladder_own", 0), ("ladder_own", 1), ("drain", None), ("core", 4),
    ("ladder_other", 0), ("ladder_other", 1),
]


def slot_of(offset):
    return offset + offset // 4 * (11 - 2 * offset)


def xor(a, b, bits):
    total = 0
    for level in range(bits):
        unit = 2**level
        total = total + (a // unit % 2 + b // unit % 2) % 2 * unit
    return total


def kernel(
    ints, amps, lists, occ, virt, out, buf, inner, dense, raw, tiles, mirror, codes, mirror_codes,
    listing, occ_s, virt_v, scale, acc,
    local, ysend, yrecv, xsend, xrecv, csend, crecv, msend, mrecv, vsend, vrecv,
):
    ia, ja, v = lax.axis_index("ia"), lax.axis_index("ja"), lax.axis_index("vert")
    x, y = ia % NX, ia // NX * 2 + v
    z, core = ja // 2, ja % 2

    def device(x_at, y_at, z_at, core_at):
        return (y_at // 2 * NX + x_at, z_at * 2 + core_at, y_at % 2)

    to_right, to_left = device((x + 1) % NX, y, z, core), device((x + 3) % NX, y, z, core)
    to_next, to_back = device(x, (y + 1) % NY, z, core), device(x, (y + 7) % NY, z, core)
    to_core = device(x, y, z, 1 - core)
    to_vert = (ia, ja, 1 - v)
    partner = xor(ia, ja, 4)
    far = ja // 8 * (1 - ja // 4 % 2)
    w = v + far * (1 - 2 * v)
    to_mirror = (partner, ja, w)
    has_mirror = ja > 0

    barrier = pltpu.get_barrier_semaphore()
    peers = [to_right, to_left, to_next, to_back, to_core]
    for peer in peers:
        pl.semaphore_signal(barrier, inc=1, device_id=peer, device_id_type=MESH)

    @pl.when(has_mirror)
    def _():
        pl.semaphore_signal(barrier, inc=1, device_id=to_mirror, device_id_type=MESH)

    fetch = [
        pltpu.make_async_copy(amps.at[0, 0], raw, local.at[0]),
        pltpu.make_async_copy(lists, listing, local.at[1]),
        pltpu.make_async_copy(ints.at[core], buf.at[0, 0, 0], local.at[2]),
        pltpu.make_async_copy(ints.at[1 - core], buf.at[1, 0, 0], local.at[3]),
        pltpu.make_async_copy(occ, occ_s, local.at[4]),
        pltpu.make_async_copy(virt, virt_v.at[0], local.at[5]),
    ]
    for copy in fetch:
        copy.start()
    @pl.when(has_mirror)
    def _():
        pl.semaphore_wait(barrier, len(peers) + 1)

    @pl.when(jnp.logical_not(has_mirror))
    def _():
        pl.semaphore_wait(barrier, len(peers))

    def send(src, dst, send_sem, recv_sem, target):
        return pltpu.make_async_remote_copy(
            src_ref=src, dst_ref=dst, send_sem=send_sem, recv_sem=recv_sem,
            device_id=target, device_id_type=MESH,
        )

    def block(n, s, r):
        rows = pl.ds(r * HALF, HALF)
        return ints.at[core, rows] if n == s == 0 else buf.at[0, n, s, rows]

    def landing(n, s, r):
        return buf.at[0, n, s, pl.ds(r * HALF, HALF)]

    def along_y(src, dst, r, index, target):
        return send(block(0, src, r), landing(0, dst, r), ysend.at[index], yrecv.at[index], target)

    ahead = [[along_y((0, 4, 5)[st], 4 + st, r, 4 * st + r, to_next) for r in range(2)] for st in range(3)]
    behind = [[along_y(st, 1 + st, r, 4 * st + 2 + r, to_back) for r in range(2)] for st in range(3)]
    ahead.append([along_y(6, 7, 0, 12, to_next), None])
    behind.append([None, along_y(3, 7, 1, 13, to_back)])

    def along_x(n, m, s, r, target):
        index = (m - 1) * 16 + s * 2 + r
        return send(block(n, s, r), landing(m, s, r), xsend.at[index], xrecv.at[index], target)

    rightward = [[along_x(0, 1, s, r, to_right) for r in range(2)] for s in range(8)]
    leftward = [[along_x(0, 2, s, r, to_left) for r in range(2)] for s in range(8)]
    relay = [[along_x(1, 3, s, 0, to_right), along_x(2, 3, s, 1, to_left)] for s in range(8)]

    def along_c(n, s, r):
        st = [st for st, slots in enumerate(STAGES) if s in slots][0]
        there = buf.at[1, n, s, pl.ds(r * HALF, HALF)]
        send(landing(n, s, r), there, csend.at[st], crecv.at[st], to_core).start()

    def from_column(st):
        for r in range(2):
            for way, s in ((ahead, 3 + st), (behind, st)):
                if st and way[st - 1][r] is not None:
                    way[st - 1][r].wait_recv()
                if st < 4 and way[st][r] is not None:
                    way[st][r].start()
                if st in (0, 4) and way is not ahead:
                    s = STAGES[st][0]
                elif st in (0, 4):
                    continue
                rightward[s][r].start()
                leftward[s][r].start()
                if st:
                    along_c(0, s, r)

    def from_sides(st):
        for r in range(2):
            for s in STAGES[st]:
                rightward[s][r].wait_recv()
                if r == 0:
                    relay[s][r].start()
                along_c(1, s, r)
                leftward[s][r].wait_recv()
                if r == 1:
                    relay[s][r].start()
                along_c(2, s, r)

    def from_across(st):
        for r in range(2):
            for s in STAGES[st]:
                relay[s][r].wait_recv()
                along_c(3, s, r)

    def whole(st):
        here = buf.at[1, slice(0 if st else 1, 4), 0 : len(STAGES[st])]
        return send(here, here, csend.at[st], crecv.at[st], to_core)

    def from_core(st):
        whole(st).wait_recv()

    def chunk(half, k):
        return pl.ds(half * 6 + 2 * k, 2)

    over = [
        send(tiles.at[chunk(w, k)], mirror.at[chunk(w, k)], msend.at[k], mrecv.at[k], to_mirror)
        for k in range(KT)
    ]
    over_codes = send(codes, mirror_codes, msend.at[KT], mrecv.at[KT], to_mirror)
    aside = [
        send(mirror.at[chunk(v, k)], mirror.at[chunk(v, k)], vsend.at[k], vrecv.at[k], to_vert)
        for k in range(KT)
    ]

    def relayout(_):
        fetch[0].wait()
        for i in range(2):
            for k in range(KT):
                tiles[pl.ds((i * KT + k) * 2, 2)] = raw[i, k].reshape(2, VB, VB)
        fetch[1].wait()
        for k in range(KT):
            codes[k : k + 1, :] = jnp.broadcast_to(listing[0, :, k : k + 1], (1, 128))

    def send_mirror(k):
        @pl.when(has_mirror)
        def _():
            if k == 0:
                over_codes.start()
            over[k].start()

        @pl.when(jnp.logical_not(has_mirror))
        def _():
            mirror[4 * k : 4 * k + 4] = tiles[4 * k : 4 * k + 4]
            mirror_codes[...] = codes[...]

    def forward_mirror(k):
        @pl.when(has_mirror)
        def _():
            over[k].wait_recv()
            aside[k].start()

    def placed(tiles, listing, i, j, tile):
        total = None
        for k in range(KT):
            factor = jnp.where(listing[k : k + 1, :] == tile, 1.0, 0.0).astype(jnp.bfloat16)
            term = tiles[(i * KT + k) * 2 + j] * factor
            total = term if total is None else total + term
        return total

    def place(i, c, d):
        return (slice(c * VB, (c + 1) * VB), slice(i * WIDE + d * VB, i * WIDE + (d + 1) * VB))

    def prepare(_):
        for i in range(2):
            for j in range(2):
                for c in range(NT):
                    for d in range(NT):
                        dense[(j, *place(i, c, d))] = placed(tiles, codes, i, j, c * NT + d)
        fetch[4].wait()
        fetch[5].wait()
        every = virt_v[0:1, :]
        own = jnp.where(v == 0, every[:, :VB], every[:, VB:])
        down = jnp.broadcast_to(own, (VB, VB)).T
        virtual = jnp.concatenate([down, down], axis=1) + every
        for i in range(2):
            for j in range(2):
                energy = occ_s[ia * 2 + i] + occ_s[partner * 2 + j]
                scale[j, i * VB : (i + 1) * VB] = 1.0 / (virtual - energy)

    def symmetrize(part):
        h = v + part * (1 - 2 * v)

        @pl.when(has_mirror)
        def _():
            if part == 0:
                over_codes.wait_recv()
            else:
                for copy in aside:
                    copy.wait_recv()

        for i in range(2):
            for c in range(NT):
                for d in range(NT):
                    at = (h, *place(i, c, d))
                    turned = placed(mirror, mirror_codes, h, i, d * NT + c)
                    total = dense[at].astype(jnp.float32) + turned.astype(jnp.float32).T
                    dense[at] = total.astype(jnp.bfloat16)

    def product(e, h, ks):
        here = slot_of(2 * e % 8)
        low, high = slot_of((2 * e - v + 8) % 8), slot_of((2 * e + 1 - v) % 8)
        which = [(k, n) for k in ks for n in range(4)]
        for q in range(0, len(which), 2):
            rows = jnp.concatenate([buf[(*which[q], here)], buf[(*which[q + 1], here)]], axis=0)
            for i in range(2):
                part_inner = jnp.dot(
                    rows, dense[h, :, i * WIDE : (i + 1) * WIDE], preferred_element_type=jnp.float32
                ).astype(jnp.bfloat16)
                for s in range(2):
                    inner[i * VB : (i + 1) * VB, (q + s) * WIDE : (q + s + 1) * WIDE] = (
                        part_inner[s * VB : (s + 1) * VB]
                    )
        factors = [jnp.concatenate([buf[(*at, low)], buf[(*at, high)]], axis=0) for at in which]
        return lax.dot_general(
            inner[:, : len(which) * WIDE], jnp.concatenate(factors, axis=1), ROWS_BY_ROWS,
            preferred_element_type=jnp.float32,
        )

    def pairs(part):
        return v + part * (1 - 2 * v)

    def ladder(index):
        h, e = pairs(index % 2), [0, 3 - 2 * v, 1 + 2 * v][index // 2]
        if index == 0:
            fetch[2].wait()
            fetch[3].wait()
        term = product(e, h, (0, 1))
        acc[h] = term if index < 2 else acc[h] + term

    def ladder_own(part):
        h = pairs(part)
        acc[h] += product(2, h, (0,))

    def ladder_other(part):
        h = pairs(part)
        result = ((acc[h] + product(2, h, (1,))) * scale[h]).astype(jnp.bfloat16)
        for i in range(2):
            out[0, 0, i, h] = result[i * VB : (i + 1) * VB]

    def drain(_):
        for copies in [*ahead, *behind, *rightward, *leftward, *relay]:
            for copy in copies:
                if copy is not None:
                    copy.wait_send()
        for st in range(4):
            whole(st).wait_send()

        @pl.when(has_mirror)
        def _():
            for copy in [*over, over_codes, *aside]:
                copy.wait_send()

    steps = {
        "column": from_column, "sides": from_sides, "across": from_across, "core": from_core,
        "mirror": send_mirror, "forward": forward_mirror, "prepare": prepare,
        "symmetrize": symmetrize, "ladder": ladder, "ladder_own": ladder_own, "ladder_other": ladder_other,
        "relayout": relayout, "drain": drain,
    }
    for name, index in ORDER:
        steps[name](index)

    whole(4).wait_send()


def on_device(amplitudes, tile_lists, integrals, occupied_energy, virtual_energy):
    occ_tile = amplitudes.shape[2]
    half_rows, width = integrals.shape[1:]
    anywhere = pl.BlockSpec(memory_space=pl.ANY)
    dma = pltpu.SemaphoreType.DMA
    by_tile = amplitudes.transpose(0, 1, 2, 4, 3, 5)
    return pl.pallas_call(
        kernel,
        out_shape=jax.ShapeDtypeStruct((1, 1, occ_tile, occ_tile, half_rows, width), jnp.bfloat16),
        in_specs=[anywhere] * 5,
        out_specs=pl.BlockSpec(memory_space=pltpu.VMEM),
        scratch_shapes=[
            pltpu.VMEM((2, NX, NY, VB, WIDE), jnp.bfloat16),
            pltpu.VMEM((2 * VB, 8 * WIDE), jnp.bfloat16),
            pltpu.VMEM((2, WIDE, 2 * WIDE), jnp.bfloat16),
            pltpu.VMEM(by_tile.shape[2:], jnp.bfloat16),
            pltpu.VMEM((PAIRS * KT, VB, VB), jnp.bfloat16),
            pltpu.VMEM((PAIRS * KT, VB, VB), jnp.bfloat16),
            pltpu.VMEM((8, 128), jnp.int32),
            pltpu.VMEM((8, 128), jnp.int32),
            pltpu.VMEM(tile_lists.shape, jnp.int32),
            pltpu.SMEM(occupied_energy.shape, jnp.float32),
            pltpu.VMEM((8, WIDE), jnp.float32),
            pltpu.VMEM((2, 2 * VB, WIDE), jnp.float32),
            pltpu.VMEM((2, 2 * VB, WIDE), jnp.float32),
            dma((6,)), dma((14,)), dma((14,)), dma((48,)), dma((48,)), dma((5,)), dma((5,)),
            dma((KT + 1,)), dma((KT + 1,)), dma((KT,)), dma((KT,)),
        ],
        compiler_params=pltpu.CompilerParams(
            collective_id=0, has_side_effects=True, vmem_limit_bytes=60 * 1024 * 1024
        ),
        name="ladder",
    )(integrals, by_tile, tile_lists, occupied_energy, virtual_energy)


def solution(mesh):
    return jax.shard_map(
        on_device,
        mesh=mesh,
        in_specs=(
            P("ia", "ja", None, None, None, None),
            P("ia", "ja", None),
            P("ia", "vert", None),
            P(),
            P(),
        ),
        out_specs=P("ia", "ja", None, None, "vert", None),
        check_vma=False,
    )
```

```python
import jax
import jax.numpy as jnp
from jax import lax
from jax.experimental import pallas as pl
from jax.experimental.pallas import tpu as pltpu
from jax.sharding import PartitionSpec as P

NX, NY = 4, 8
NT = 2
VB = 128
KT = 3
WIDE = 256
PAIRS = 4
HALF = VB // 2
MESH = pl.DeviceIdType.MESH
ROWS_BY_ROWS = (((1,), (1,)), ((), ()))

STAGES = [(0,), (1, 4), (2, 5), (3, 6), (7,)]
ORDER = [
    ("column", 0), ("relayout", None), ("mirror", 0), ("prepare", None), ("column", 1), ("mirror", 1),
    ("sides", 0), ("column", 2), ("mirror", 2), ("sides", 1), ("forward", 0), ("column", 3), ("across", 0),
    ("sides", 2), ("forward", 1), ("column", 4), ("across", 1), ("forward", 2), ("core", 0), ("core", 1),
    ("symmetrize", 0), ("sides", 3), ("across", 2), ("ladder", 0), ("sides", 4), ("core", 2), ("ladder", 2),
    ("symmetrize", 1), ("across", 3), ("ladder", 1), ("ladder", 3), ("core", 3), ("across", 4),
    ("ladder", 4), ("ladder", 5), ("ladder_own", 0), ("ladder_own", 1), ("drain", None), ("core", 4),
    ("ladder_other", 0), ("ladder_other", 1),
]


def slot_of(offset):
    return offset + offset // 4 * (11 - 2 * offset)


def xor(a, b, bits):
    total = 0
    for level in range(bits):
        unit = 2**level
        total = total + (a // unit % 2 + b // unit % 2) % 2 * unit
    return total


def kernel(
    ints, amps, lists, occ, virt, out, buf, inner, dense, raw, tiles, mirror, codes, mirror_codes,
    listing, occ_s, virt_v, scale, acc,
    local, ysend, yrecv, xsend, xrecv, csend, crecv, msend, mrecv, vsend, vrecv,
):
    ia, ja, v = lax.axis_index("ia"), lax.axis_index("ja"), lax.axis_index("vert")
    x, y = ia % NX, ia // NX * 2 + v
    z, core = ja // 2, ja % 2

    def device(x_at, y_at, z_at, core_at):
        return (y_at // 2 * NX + x_at, z_at * 2 + core_at, y_at % 2)

    to_right, to_left = device((x + 1) % NX, y, z, core), device((x + 3) % NX, y, z, core)
    to_next, to_back = device(x, (y + 1) % NY, z, core), device(x, (y + 7) % NY, z, core)
    to_core = device(x, y, z, 1 - core)
    to_vert = (ia, ja, 1 - v)
    partner = xor(ia, ja, 4)
    far = ja // 8 * (1 - ja // 4 % 2)
    w = v + far * (1 - 2 * v)
    to_mirror = (partner, ja, w)
    has_mirror = ja > 0

    barrier = pltpu.get_barrier_semaphore()
    peers = [to_right, to_left, to_next, to_back, to_core]
    for peer in peers:
        pl.semaphore_signal(barrier, inc=1, device_id=peer, device_id_type=MESH)

    @pl.when(has_mirror)
    def _():
        pl.semaphore_signal(barrier, inc=1, device_id=to_mirror, device_id_type=MESH)

    fetch = [
        pltpu.make_async_copy(amps.at[0, 0], raw, local.at[0]),
        pltpu.make_async_copy(lists, listing, local.at[1]),
        pltpu.make_async_copy(ints.at[core], buf.at[0, 0, 0], local.at[2]),
        pltpu.make_async_copy(ints.at[1 - core], buf.at[1, 0, 0], local.at[3]),
        pltpu.make_async_copy(occ, occ_s, local.at[4]),
        pltpu.make_async_copy(virt, virt_v.at[0], local.at[5]),
    ]
    for copy in fetch:
        copy.start()
    @pl.when(has_mirror)
    def _():
        pl.semaphore_wait(barrier, len(peers) + 1)

    @pl.when(jnp.logical_not(has_mirror))
    def _():
        pl.semaphore_wait(barrier, len(peers))

    def send(src, dst, send_sem, recv_sem, target):
        return pltpu.make_async_remote_copy(
            src_ref=src, dst_ref=dst, send_sem=send_sem, recv_sem=recv_sem,
            device_id=target, device_id_type=MESH,
        )

    def block(n, s, r):
        rows = pl.ds(r * HALF, HALF)
        return ints.at[core, rows] if n == s == 0 else buf.at[0, n, s, rows]

    def landing(n, s, r):
        return buf.at[0, n, s, pl.ds(r * HALF, HALF)]

    def along_y(src, dst, r, index, target):
        return send(block(0, src, r), landing(0, dst, r), ysend.at[index], yrecv.at[index], target)

    ahead = [[along_y((0, 4, 5)[st], 4 + st, r, 4 * st + r, to_next) for r in range(2)] for st in range(3)]
    behind = [[along_y(st, 1 + st, r, 4 * st + 2 + r, to_back) for r in range(2)] for st in range(3)]
    ahead.append([along_y(6, 7, 0, 12, to_next), None])
    behind.append([None, along_y(3, 7, 1, 13, to_back)])

    def along_x(n, m, s, r, target):
        index = (m - 1) * 16 + s * 2 + r
        return send(block(n, s, r), landing(m, s, r), xsend.at[index], xrecv.at[index], target)

    rightward = [[along_x(0, 1, s, r, to_right) for r in range(2)] for s in range(8)]
    leftward = [[along_x(0, 2, s, r, to_left) for r in range(2)] for s in range(8)]
    relay = [[along_x(1, 3, s, 0, to_right), along_x(2, 3, s, 1, to_left)] for s in range(8)]

    def along_c(n, s, r):
        st = [st for st, slots in enumerate(STAGES) if s in slots][0]
        there = buf.at[1, n, s, pl.ds(r * HALF, HALF)]
        send(landing(n, s, r), there, csend.at[st], crecv.at[st], to_core).start()

    def from_column(st):
        for r in range(2):
            for way, s in ((ahead, 3 + st), (behind, st)):
                if st and way[st - 1][r] is not None:
                    way[st - 1][r].wait_recv()
                if st < 4 and way[st][r] is not None:
                    way[st][r].start()
                if st in (0, 4) and way is not ahead:
                    s = STAGES[st][0]
                elif st in (0, 4):
                    continue
                rightward[s][r].start()
                leftward[s][r].start()
                if st:
                    along_c(0, s, r)

    def from_sides(st):
        for r in range(2):
            for s in STAGES[st]:
                rightward[s][r].wait_recv()
                if r == 0:
                    relay[s][r].start()
                along_c(1, s, r)
                leftward[s][r].wait_recv()
                if r == 1:
                    relay[s][r].start()
                along_c(2, s, r)

    def from_across(st):
        for r in range(2):
            for s in STAGES[st]:
                relay[s][r].wait_recv()
                along_c(3, s, r)

    def whole(st):
        here = buf.at[1, slice(0 if st else 1, 4), 0 : len(STAGES[st])]
        return send(here, here, csend.at[st], crecv.at[st], to_core)

    def from_core(st):
        whole(st).wait_recv()

    def chunk(half, k):
        return pl.ds(half * 6 + 2 * k, 2)

    over = [
        send(tiles.at[chunk(w, k)], mirror.at[chunk(w, k)], msend.at[k], mrecv.at[k], to_mirror)
        for k in range(KT)
    ]
    over_codes = send(codes, mirror_codes, msend.at[KT], mrecv.at[KT], to_mirror)
    aside = [
        send(mirror.at[chunk(v, k)], mirror.at[chunk(v, k)], vsend.at[k], vrecv.at[k], to_vert)
        for k in range(KT)
    ]

    def relayout(_):
        fetch[0].wait()
        for i in range(2):
            for k in range(KT):
                tiles[pl.ds((i * KT + k) * 2, 2)] = raw[i, k].reshape(2, VB, VB)
        fetch[1].wait()
        for k in range(KT):
            codes[k : k + 1, :] = jnp.broadcast_to(listing[0, :, k : k + 1], (1, 128))

    def send_mirror(k):
        @pl.when(has_mirror)
        def _():
            if k == 0:
                over_codes.start()
            over[k].start()

        @pl.when(jnp.logical_not(has_mirror))
        def _():
            mirror[4 * k : 4 * k + 4] = tiles[4 * k : 4 * k + 4]
            mirror_codes[...] = codes[...]

    def forward_mirror(k):
        @pl.when(has_mirror)
        def _():
            over[k].wait_recv()
            aside[k].start()

    def placed(tiles, listing, i, j, tile):
        total = None
        for k in range(KT):
            factor = jnp.where(listing[k : k + 1, :] == tile, 1.0, 0.0).astype(jnp.bfloat16)
            term = tiles[(i * KT + k) * 2 + j] * factor
            total = term if total is None else total + term
        return total

    def place(i, c, d):
        return (slice(c * VB, (c + 1) * VB), slice(i * WIDE + d * VB, i * WIDE + (d + 1) * VB))

    def prepare(_):
        for i in range(2):
            for j in range(2):
                for c in range(NT):
                    for d in range(NT):
                        dense[(j, *place(i, c, d))] = placed(tiles, codes, i, j, c * NT + d)
        fetch[4].wait()
        fetch[5].wait()
        every = virt_v[0:1, :]
        own = jnp.where(v == 0, every[:, :VB], every[:, VB:])
        down = jnp.broadcast_to(own, (VB, VB)).T
        virtual = jnp.concatenate([down, down], axis=1) + every
        for i in range(2):
            for j in range(2):
                energy = occ_s[ia * 2 + i] + occ_s[partner * 2 + j]
                scale[j, i * VB : (i + 1) * VB] = 1.0 / (virtual - energy)

    def symmetrize(part):
        h = v + part * (1 - 2 * v)

        @pl.when(has_mirror)
        def _():
            if part == 0:
                over_codes.wait_recv()
            else:
                for copy in aside:
                    copy.wait_recv()

        for i in range(2):
            for c in range(NT):
                for d in range(NT):
                    at = (h, *place(i, c, d))
                    turned = placed(mirror, mirror_codes, h, i, d * NT + c)
                    total = dense[at].astype(jnp.float32) + turned.astype(jnp.float32).T
                    dense[at] = total.astype(jnp.bfloat16)

    def product(e, h, ks):
        here = slot_of(2 * e % 8)
        low, high = slot_of((2 * e - v + 8) % 8), slot_of((2 * e + 1 - v) % 8)
        which = [(k, n) for k in ks for n in range(4)]
        for q in range(0, len(which), 2):
            rows = jnp.concatenate([buf[(*which[q], here)], buf[(*which[q + 1], here)]], axis=0)
            for i in range(2):
                part_inner = jnp.dot(
                    rows, dense[h, :, i * WIDE : (i + 1) * WIDE], preferred_element_type=jnp.float32
                ).astype(jnp.bfloat16)
                for s in range(2):
                    inner[i * VB : (i + 1) * VB, (q + s) * WIDE : (q + s + 1) * WIDE] = (
                        part_inner[s * VB : (s + 1) * VB]
                    )
        factors = [jnp.concatenate([buf[(*at, low)], buf[(*at, high)]], axis=0) for at in which]
        return lax.dot_general(
            inner[:, : len(which) * WIDE], jnp.concatenate(factors, axis=1), ROWS_BY_ROWS,
            preferred_element_type=jnp.float32,
        )

    def pairs(part):
        return v + part * (1 - 2 * v)

    def ladder(index):
        h, e = pairs(index % 2), [0, 3 - 2 * v, 1 + 2 * v][index // 2]
        if index == 0:
            fetch[2].wait()
            fetch[3].wait()
        term = product(e, h, (0, 1))
        acc[h] = term if index < 2 else acc[h] + term

    def ladder_own(part):
        h = pairs(part)
        acc[h] += product(2, h, (0,))

    def ladder_other(part):
        h = pairs(part)
        result = ((acc[h] + product(2, h, (1,))) * scale[h]).astype(jnp.bfloat16)
        for i in range(2):
            out[0, 0, i, h] = result[i * VB : (i + 1) * VB]

    def drain(_):
        for copies in [*ahead, *behind, *rightward, *leftward, *relay]:
            for copy in copies:
                if copy is not None:
                    copy.wait_send()
        for st in range(4):
            whole(st).wait_send()

        @pl.when(has_mirror)
        def _():
            for copy in [*over, over_codes, *aside]:
                copy.wait_send()

    steps = {
        "column": from_column, "sides": from_sides, "across": from_across, "core": from_core,
        "mirror": send_mirror, "forward": forward_mirror, "prepare": prepare,
        "symmetrize": symmetrize, "ladder": ladder, "ladder_own": ladder_own, "ladder_other": ladder_other,
        "relayout": relayout, "drain": drain,
    }
    for name, index in ORDER:
        steps[name](index)

    whole(4).wait_send()


def on_device(amplitudes, tile_lists, integrals, occupied_energy, virtual_energy):
    occ_tile = amplitudes.shape[2]
    half_rows, width = integrals.shape[1:]
    anywhere = pl.BlockSpec(memory_space=pl.ANY)
    dma = pltpu.SemaphoreType.DMA
    by_tile = amplitudes.transpose(0, 1, 2, 4, 3, 5)
    return pl.pallas_call(
        kernel,
        out_shape=jax.ShapeDtypeStruct((1, 1, occ_tile, occ_tile, half_rows, width), jnp.bfloat16),
        in_specs=[anywhere] * 5,
        out_specs=pl.BlockSpec(memory_space=pltpu.VMEM),
        scratch_shapes=[
            pltpu.VMEM((2, NX, NY, VB, WIDE), jnp.bfloat16),
            pltpu.VMEM((2 * VB, 8 * WIDE), jnp.bfloat16),
            pltpu.VMEM((2, WIDE, 2 * WIDE), jnp.bfloat16),
            pltpu.VMEM(by_tile.shape[2:], jnp.bfloat16),
            pltpu.VMEM((PAIRS * KT, VB, VB), jnp.bfloat16),
            pltpu.VMEM((PAIRS * KT, VB, VB), jnp.bfloat16),
            pltpu.VMEM((8, 128), jnp.int32),
            pltpu.VMEM((8, 128), jnp.int32),
            pltpu.VMEM(tile_lists.shape, jnp.int32),
            pltpu.SMEM(occupied_energy.shape, jnp.float32),
            pltpu.VMEM((8, WIDE), jnp.float32),
            pltpu.VMEM((2, 2 * VB, WIDE), jnp.float32),
            pltpu.VMEM((2, 2 * VB, WIDE), jnp.float32),
            dma((6,)), dma((14,)), dma((14,)), dma((48,)), dma((48,)), dma((5,)), dma((5,)),
            dma((KT + 1,)), dma((KT + 1,)), dma((KT,)), dma((KT,)),
        ],
        compiler_params=pltpu.CompilerParams(
            collective_id=0, has_side_effects=True, vmem_limit_bytes=60 * 1024 * 1024
        ),
        name="ladder",
    )(integrals, by_tile, tile_lists, occupied_energy, virtual_energy)


def solution(mesh):
    return jax.shard_map(
        on_device,
        mesh=mesh,
        in_specs=(
            P("ia", "ja", None, None, None, None),
            P("ia", "ja", None),
            P("ia", "vert", None),
            P(),
            P(),
        ),
        out_specs=P("ia", "ja", None, None, "vert", None),
        check_vma=False,
    )
```

```python
import jax
import jax.numpy as jnp
from jax import lax
from jax.experimental import pallas as pl
from jax.experimental.pallas import tpu as pltpu
from jax.sharding import PartitionSpec as P

NX, NY = 4, 8
NT = 2
VB = 128
KT = 3
WIDE = 256
PAIRS = 4
HALF = VB // 2
MESH = pl.DeviceIdType.MESH
ROWS_BY_ROWS = (((1,), (1,)), ((), ()))

STAGES = [(0,), (1, 4), (2, 5), (3, 6), (7,)]
ORDER = [
    ("column", 0), ("relayout", None), ("mirror", 0), ("column", 1), ("mirror", 1), ("prepare", None),
    ("sides", 0), ("column", 2), ("mirror", 2), ("sides", 1), ("forward", 0), ("column", 3), ("across", 0),
    ("forward", 1), ("sides", 2), ("column", 4), ("forward", 2), ("across", 1), ("core", 0), ("core", 1),
    ("symmetrize", 0), ("sides", 3), ("across", 2), ("ladder", 0), ("sides", 4), ("core", 2), ("ladder", 2),
    ("symmetrize", 1), ("across", 3), ("ladder", 1), ("ladder", 3), ("core", 3), ("across", 4),
    ("ladder", 4), ("ladder", 5), ("ladder_own", 0), ("ladder_own", 1), ("drain", None), ("core", 4),
    ("ladder_other", 0), ("ladder_other", 1),
]


def slot_of(offset):
    return offset + offset // 4 * (11 - 2 * offset)


def xor(a, b, bits):
    total = 0
    for level in range(bits):
        unit = 2**level
        total = total + (a // unit % 2 + b // unit % 2) % 2 * unit
    return total


def kernel(
    ints, amps, lists, occ, virt, out, buf, inner, dense, raw, tiles, mirror, codes, mirror_codes,
    listing, occ_s, virt_v, scale, acc,
    local, ysend, yrecv, xsend, xrecv, csend, crecv, msend, mrecv, vsend, vrecv,
):
    ia, ja, v = lax.axis_index("ia"), lax.axis_index("ja"), lax.axis_index("vert")
    x, y = ia % NX, ia // NX * 2 + v
    z, core = ja // 2, ja % 2

    def device(x_at, y_at, z_at, core_at):
        return (y_at // 2 * NX + x_at, z_at * 2 + core_at, y_at % 2)

    to_right, to_left = device((x + 1) % NX, y, z, core), device((x + 3) % NX, y, z, core)
    to_next, to_back = device(x, (y + 1) % NY, z, core), device(x, (y + 7) % NY, z, core)
    to_core = device(x, y, z, 1 - core)
    to_vert = (ia, ja, 1 - v)
    partner = xor(ia, ja, 4)
    far = ja // 8 * (1 - ja // 4 % 2)
    w = v + far * (1 - 2 * v)
    to_mirror = (partner, ja, w)
    has_mirror = ja > 0

    barrier = pltpu.get_barrier_semaphore()
    peers = [to_right, to_left, to_next, to_back, to_core]
    for peer in peers:
        pl.semaphore_signal(barrier, inc=1, device_id=peer, device_id_type=MESH)

    @pl.when(has_mirror)
    def _():
        pl.semaphore_signal(barrier, inc=1, device_id=to_mirror, device_id_type=MESH)

    fetch = [
        pltpu.make_async_copy(amps.at[0, 0], raw, local.at[0]),
        pltpu.make_async_copy(lists, listing, local.at[1]),
        pltpu.make_async_copy(ints.at[core], buf.at[0, 0, 0], local.at[2]),
        pltpu.make_async_copy(ints.at[1 - core], buf.at[1, 0, 0], local.at[3]),
        pltpu.make_async_copy(occ, occ_s, local.at[4]),
        pltpu.make_async_copy(virt, virt_v.at[0], local.at[5]),
    ]
    for copy in fetch:
        copy.start()
    @pl.when(has_mirror)
    def _():
        pl.semaphore_wait(barrier, len(peers) + 1)

    @pl.when(jnp.logical_not(has_mirror))
    def _():
        pl.semaphore_wait(barrier, len(peers))

    def send(src, dst, send_sem, recv_sem, target):
        return pltpu.make_async_remote_copy(
            src_ref=src, dst_ref=dst, send_sem=send_sem, recv_sem=recv_sem,
            device_id=target, device_id_type=MESH,
        )

    def block(n, s, r):
        rows = pl.ds(r * HALF, HALF)
        return ints.at[core, rows] if n == s == 0 else buf.at[0, n, s, rows]

    def landing(n, s, r):
        return buf.at[0, n, s, pl.ds(r * HALF, HALF)]

    def along_y(src, dst, r, index, target):
        return send(block(0, src, r), landing(0, dst, r), ysend.at[index], yrecv.at[index], target)

    ahead = [[along_y((0, 4, 5)[st], 4 + st, r, 4 * st + r, to_next) for r in range(2)] for st in range(3)]
    behind = [[along_y(st, 1 + st, r, 4 * st + 2 + r, to_back) for r in range(2)] for st in range(3)]
    ahead.append([along_y(6, 7, 0, 12, to_next), None])
    behind.append([None, along_y(3, 7, 1, 13, to_back)])

    def along_x(n, m, s, r, target):
        index = (m - 1) * 16 + s * 2 + r
        return send(block(n, s, r), landing(m, s, r), xsend.at[index], xrecv.at[index], target)

    rightward = [[along_x(0, 1, s, r, to_right) for r in range(2)] for s in range(8)]
    leftward = [[along_x(0, 2, s, r, to_left) for r in range(2)] for s in range(8)]
    relay = [[along_x(1, 3, s, 0, to_right), along_x(2, 3, s, 1, to_left)] for s in range(8)]

    def along_c(n, s, r):
        st = [st for st, slots in enumerate(STAGES) if s in slots][0]
        there = buf.at[1, n, s, pl.ds(r * HALF, HALF)]
        send(landing(n, s, r), there, csend.at[st], crecv.at[st], to_core).start()

    def from_column(st):
        for r in range(2):
            for way, s in ((ahead, 3 + st), (behind, st)):
                if st and way[st - 1][r] is not None:
                    way[st - 1][r].wait_recv()
                if st < 4 and way[st][r] is not None:
                    way[st][r].start()
                if st in (0, 4) and way is not ahead:
                    s = STAGES[st][0]
                elif st in (0, 4):
                    continue
                rightward[s][r].start()
                leftward[s][r].start()
                if st:
                    along_c(0, s, r)

    def from_sides(st):
        for r in range(2):
            for s in STAGES[st]:
                rightward[s][r].wait_recv()
                if r == 0:
                    relay[s][r].start()
                along_c(1, s, r)
                leftward[s][r].wait_recv()
                if r == 1:
                    relay[s][r].start()
                along_c(2, s, r)

    def from_across(st):
        for r in range(2):
            for s in STAGES[st]:
                relay[s][r].wait_recv()
                along_c(3, s, r)

    def whole(st):
        here = buf.at[1, slice(0 if st else 1, 4), 0 : len(STAGES[st])]
        return send(here, here, csend.at[st], crecv.at[st], to_core)

    def from_core(st):
        whole(st).wait_recv()

    def chunk(half, k):
        return pl.ds(half * 6 + 2 * k, 2)

    over = [
        send(tiles.at[chunk(w, k)], mirror.at[chunk(w, k)], msend.at[k], mrecv.at[k], to_mirror)
        for k in range(KT)
    ]
    over_codes = send(codes, mirror_codes, msend.at[KT], mrecv.at[KT], to_mirror)
    aside = [
        send(mirror.at[chunk(v, k)], mirror.at[chunk(v, k)], vsend.at[k], vrecv.at[k], to_vert)
        for k in range(KT)
    ]

    def relayout(_):
        fetch[0].wait()
        for i in range(2):
            for k in range(KT):
                tiles[pl.ds((i * KT + k) * 2, 2)] = raw[i, k].reshape(2, VB, VB)
        fetch[1].wait()
        for k in range(KT):
            codes[k : k + 1, :] = jnp.broadcast_to(listing[0, :, k : k + 1], (1, 128))

    def send_mirror(k):
        @pl.when(has_mirror)
        def _():
            if k == 0:
                over_codes.start()
            over[k].start()

        @pl.when(jnp.logical_not(has_mirror))
        def _():
            mirror[4 * k : 4 * k + 4] = tiles[4 * k : 4 * k + 4]
            mirror_codes[...] = codes[...]

    def forward_mirror(k):
        @pl.when(has_mirror)
        def _():
            over[k].wait_recv()
            aside[k].start()

    def placed(tiles, listing, i, j, tile):
        total = None
        for k in range(KT):
            factor = jnp.where(listing[k : k + 1, :] == tile, 1.0, 0.0).astype(jnp.bfloat16)
            term = tiles[(i * KT + k) * 2 + j] * factor
            total = term if total is None else total + term
        return total

    def place(i, c, d):
        return (slice(c * VB, (c + 1) * VB), slice(i * WIDE + d * VB, i * WIDE + (d + 1) * VB))

    def prepare(_):
        for i in range(2):
            for j in range(2):
                for c in range(NT):
                    for d in range(NT):
                        dense[(j, *place(i, c, d))] = placed(tiles, codes, i, j, c * NT + d)
        fetch[4].wait()
        fetch[5].wait()
        every = virt_v[0:1, :]
        own = jnp.where(v == 0, every[:, :VB], every[:, VB:])
        down = jnp.broadcast_to(own, (VB, VB)).T
        virtual = jnp.concatenate([down, down], axis=1) + every
        for i in range(2):
            for j in range(2):
                energy = occ_s[ia * 2 + i] + occ_s[partner * 2 + j]
                scale[j, i * VB : (i + 1) * VB] = 1.0 / (virtual - energy)

    def symmetrize(part):
        h = v + part * (1 - 2 * v)

        @pl.when(has_mirror)
        def _():
            if part == 0:
                over_codes.wait_recv()
            else:
                for copy in aside:
                    copy.wait_recv()

        for i in range(2):
            for c in range(NT):
                for d in range(NT):
                    at = (h, *place(i, c, d))
                    turned = placed(mirror, mirror_codes, h, i, d * NT + c)
                    total = dense[at].astype(jnp.float32) + turned.astype(jnp.float32).T
                    dense[at] = total.astype(jnp.bfloat16)

    def product(e, h, ks):
        here = slot_of(2 * e % 8)
        low, high = slot_of((2 * e - v + 8) % 8), slot_of((2 * e + 1 - v) % 8)
        which = [(k, n) for k in ks for n in range(4)]
        for q in range(0, len(which), 2):
            rows = jnp.concatenate([buf[(*which[q], here)], buf[(*which[q + 1], here)]], axis=0)
            for i in range(2):
                part_inner = jnp.dot(
                    rows, dense[h, :, i * WIDE : (i + 1) * WIDE], preferred_element_type=jnp.float32
                ).astype(jnp.bfloat16)
                for s in range(2):
                    inner[i * VB : (i + 1) * VB, (q + s) * WIDE : (q + s + 1) * WIDE] = (
                        part_inner[s * VB : (s + 1) * VB]
                    )
        factors = [jnp.concatenate([buf[(*at, low)], buf[(*at, high)]], axis=0) for at in which]
        return lax.dot_general(
            inner[:, : len(which) * WIDE], jnp.concatenate(factors, axis=1), ROWS_BY_ROWS,
            preferred_element_type=jnp.float32,
        )

    def pairs(part):
        return v + part * (1 - 2 * v)

    def ladder(index):
        h, e = pairs(index % 2), [0, 3 - 2 * v, 1 + 2 * v][index // 2]
        if index == 0:
            fetch[2].wait()
            fetch[3].wait()
        term = product(e, h, (0, 1))
        acc[h] = term if index < 2 else acc[h] + term

    def ladder_own(part):
        h = pairs(part)
        acc[h] += product(2, h, (0,))

    def ladder_other(part):
        h = pairs(part)
        result = ((acc[h] + product(2, h, (1,))) * scale[h]).astype(jnp.bfloat16)
        for i in range(2):
            out[0, 0, i, h] = result[i * VB : (i + 1) * VB]

    def drain(_):
        for copies in [*ahead, *behind, *rightward, *leftward, *relay]:
            for copy in copies:
                if copy is not None:
                    copy.wait_send()
        for st in range(4):
            whole(st).wait_send()

        @pl.when(has_mirror)
        def _():
            for copy in [*over, over_codes, *aside]:
                copy.wait_send()

    steps = {
        "column": from_column, "sides": from_sides, "across": from_across, "core": from_core,
        "mirror": send_mirror, "forward": forward_mirror, "prepare": prepare,
        "symmetrize": symmetrize, "ladder": ladder, "ladder_own": ladder_own, "ladder_other": ladder_other,
        "relayout": relayout, "drain": drain,
    }
    for name, index in ORDER:
        steps[name](index)

    whole(4).wait_send()


def on_device(amplitudes, tile_lists, integrals, occupied_energy, virtual_energy):
    occ_tile = amplitudes.shape[2]
    half_rows, width = integrals.shape[1:]
    anywhere = pl.BlockSpec(memory_space=pl.ANY)
    dma = pltpu.SemaphoreType.DMA
    by_tile = amplitudes.transpose(0, 1, 2, 4, 3, 5)
    return pl.pallas_call(
        kernel,
        out_shape=jax.ShapeDtypeStruct((1, 1, occ_tile, occ_tile, half_rows, width), jnp.bfloat16),
        in_specs=[anywhere] * 5,
        out_specs=pl.BlockSpec(memory_space=pltpu.VMEM),
        scratch_shapes=[
            pltpu.VMEM((2, NX, NY, VB, WIDE), jnp.bfloat16),
            pltpu.VMEM((2 * VB, 8 * WIDE), jnp.bfloat16),
            pltpu.VMEM((2, WIDE, 2 * WIDE), jnp.bfloat16),
            pltpu.VMEM(by_tile.shape[2:], jnp.bfloat16),
            pltpu.VMEM((PAIRS * KT, VB, VB), jnp.bfloat16),
            pltpu.VMEM((PAIRS * KT, VB, VB), jnp.bfloat16),
            pltpu.VMEM((8, 128), jnp.int32),
            pltpu.VMEM((8, 128), jnp.int32),
            pltpu.VMEM(tile_lists.shape, jnp.int32),
            pltpu.SMEM(occupied_energy.shape, jnp.float32),
            pltpu.VMEM((8, WIDE), jnp.float32),
            pltpu.VMEM((2, 2 * VB, WIDE), jnp.float32),
            pltpu.VMEM((2, 2 * VB, WIDE), jnp.float32),
            dma((6,)), dma((14,)), dma((14,)), dma((48,)), dma((48,)), dma((5,)), dma((5,)),
            dma((KT + 1,)), dma((KT + 1,)), dma((KT,)), dma((KT,)),
        ],
        compiler_params=pltpu.CompilerParams(
            collective_id=0, has_side_effects=True, vmem_limit_bytes=60 * 1024 * 1024
        ),
        name="ladder",
    )(integrals, by_tile, tile_lists, occupied_energy, virtual_energy)


def solution(mesh):
    return jax.shard_map(
        on_device,
        mesh=mesh,
        in_specs=(
            P("ia", "ja", None, None, None, None),
            P("ia", "ja", None),
            P("ia", "vert", None),
            P(),
            P(),
        ),
        out_specs=P("ia", "ja", None, None, "vert", None),
        check_vma=False,
    )
```
